256 devices in a mesh: dom: 32 (over y_lo, z, core), rep: 8 (over y_hi, x).
Axes of the slice: x: 4, y: 4 (y_hi: 2, y_lo: 2; y = y_hi * 2 + y_lo), z: 8, core: 2. Of those that a mesh axis runs over, the one named last changes fastest.
Arguments:
- features: bfloat16 [32768, 128], P('dom'), may hold values from -6 to 6
- tile_values: bfloat16 [32, 8, 32, 128, 128], P('dom', 'rep'), may hold values from 0 to 0.026977539
- tile_rows: int32 [32, 8, 32], P('dom', 'rep'), may hold values from 0 to 7, as said below
- tile_cols: int32 [32, 8, 32], P('dom', 'rep'), may hold values from 0 to 255, as said below
- tile_count: int32 [32, 8], P('dom', 'rep'), may hold values from 4 to 32, as said below
- weight: bfloat16 [128, 128], replicated, may hold values from -0.5 to 0.5
- bias: float32 [128], replicated, may hold values from -3 to 3
- cotangent: bfloat16 [32768, 128], P('dom'), may hold values from -6 to 6
Outputs:
- activations: bfloat16 [32768, 128], P('dom')
- feature_grad: float32 [32768, 128], P('dom')
- weight_grad: float32 [128, 128], replicated
- bias_grad: float32 [128], replicated
The draws below stay inside these ranges and needn't reach their ends.
Inputs may be any that keep to these rules, and one draw needn't show every extreme that they name: `tile_rows`: row tile of a slot within its node block; every slot, live or not, holds an index in range. `tile_cols`: column tile of a slot; the slots of all devices of one node block name distinct (row tile, column tile) positions. The first tile_count slots of a device are live, the rest are ignored; some device has all 32 slots live.
All inputs are finite; a program needn't handle non-finite values.
Results may differ from the reference program's by a relative error of at most 0.007.
Values may be sent and summed in bfloat16 or wider, within the bound.
No kernel may reach another device: no remote copies, remote signals or barrier semaphores. Data moves between devices by JAX's collectives and lax.ppermute only.
A program may use at most 64 MiB of HBM per device.

```python
import jax
import jax.numpy as jnp
from jax import lax

F = 128
H = 128
TILE = 128
ROWS = 1024
MAXT = 32
NODES = 32768
N_DOM = 32
N_REP = 8


def tile_layout(key):
    row_tiles = ROWS // TILE
    col_tiles = ROWS * N_DOM // TILE
    places = row_tiles * col_tiles
    keys = jax.random.split(key, N_DOM)
    orders = jax.vmap(lambda k: jax.random.permutation(k, places))(keys)
    chosen = orders[:, :N_REP * MAXT].reshape(N_DOM, N_REP, MAXT).astype(jnp.int32)
    return ((chosen // col_tiles).astype(jnp.int32), (chosen % col_tiles).astype(jnp.int32))


def draw_tile_rows(key, part):
    rows_part, cols_part = tile_layout(key)
    return rows_part


def draw_tile_cols(key, part):
    rows_part, cols_part = tile_layout(key)
    return cols_part


def draw_tile_count(key, part):
    key = jax.random.fold_in(key, 13)
    first, second = jax.random.split(key)
    counts = jax.random.randint(first, (N_DOM * N_REP,), MAXT // 8, MAXT + 1).astype(jnp.int32)
    busiest = jax.random.randint(second, (), 0, N_DOM * N_REP)
    counts = jnp.where(jnp.arange(N_DOM * N_REP) == busiest, MAXT, counts).astype(jnp.int32)
    return counts.reshape(N_DOM, N_REP)


def levels(stream_key, extent, shards, smallest, largest):
    def one(axis_at, blocks):
        steps = jax.random.uniform(jax.random.fold_in(jax.random.fold_in(stream_key, 6), axis_at), (blocks,), jnp.float32, smallest / len(shards), largest / len(shards))
        return jnp.repeat(jnp.exp(steps), extent[axis_at] // blocks).reshape((-1,) + (1,) * (len(extent) - axis_at - 1))

    level = one(*shards[0])
    for cut in shards[1:]:
        level = level * one(*cut)
    return level


def scatter_about(stream_key, dims, spread, most, cuts=(), held_as=jnp.bfloat16):
    array = spread * jax.random.normal(stream_key, dims, jnp.float32)
    if cuts:
        array = array * levels(stream_key, dims, cuts, -0.22, 0.18)
    return jnp.clip(array, -most, most).astype(held_as)


def setup_inputs(seed: int = 0) -> dict:
    splits = jax.random.split(jax.random.key(seed), 9)
    features = scatter_about(splits[0], (NODES, F), 1.0, 6.0, ((0, 32),))
    tile_values = jnp.clip(0.026977539 * jax.random.uniform(splits[1], (N_DOM, N_REP, MAXT, TILE, TILE), jnp.float32) ** levels(splits[1], (N_DOM, N_REP, MAXT, TILE, TILE), ((0, 32), (1, 8)), -0.2, 0.2), 0.0, 0.026977539).astype(jnp.bfloat16)
    tile_rows = draw_tile_rows(jax.random.fold_in(splits[8], 71), 0)
    tile_cols = draw_tile_cols(jax.random.fold_in(splits[8], 71), 0)
    tile_count = draw_tile_count(jax.random.fold_in(splits[8], 71), 0)
    weight = scatter_about(splits[5], (F, H), F ** -0.5, 0.5)
    bias = scatter_about(splits[6], (H,), 0.5, 3.0, (), jnp.float32)
    cotangent = scatter_about(splits[7], (NODES, H), 1.0, 6.0, ((0, 32),))
    return {"features": features, "tile_values": tile_values, "tile_rows": tile_rows, "tile_cols": tile_cols, "tile_count": tile_count, "weight": weight, "bias": bias, "cotangent": cotangent}


def gelu_tanh(v):
    return jax.nn.gelu(v, approximate=True)

def reference(features, tile_values, tile_rows, tile_cols, tile_count, weight, bias, cotangent):
    groups = N_DOM * N_REP
    values = tile_values.reshape(groups, MAXT, TILE, TILE)
    group_index = jnp.arange(groups, dtype=jnp.int32)
    block_of = (group_index // N_REP).astype(jnp.int32)
    row_tiles = (block_of[:, None] * (ROWS // TILE) + tile_rows.reshape(groups, MAXT)).astype(jnp.int32)
    col_tiles = tile_cols.reshape(groups, MAXT).astype(jnp.int32)
    slot_index = jnp.arange(MAXT, dtype=jnp.int32)
    alive = (slot_index[None, :] < tile_count.reshape(groups)[:, None]).astype(jnp.float32)
    feature_tiles = features.reshape(NODES // TILE, TILE, F)

    def forward_step(acc, item):
        tiles, rws, cls, live = item
        sources = feature_tiles[cls]
        prod = jnp.einsum('sik,skf->sif', tiles.astype(jnp.float32), sources.astype(jnp.float32))
        prod = prod * live[:, None, None]
        return (acc.at[rws].add(prod), None)
    start = jnp.zeros((NODES // TILE, TILE, F), jnp.float32)
    summed, _ = lax.scan(forward_step, start, (values, row_tiles, col_tiles, alive))
    aggregated = summed.reshape(NODES, F).astype(jnp.bfloat16)
    preact = jnp.dot(aggregated, weight, preferred_element_type=jnp.float32) + bias
    activations = gelu_tanh(preact).astype(jnp.bfloat16)
    _, pullback = jax.vjp(gelu_tanh, preact)
    delta = pullback(cotangent.astype(jnp.float32))[0].astype(jnp.bfloat16)
    weight_grad = jnp.dot(aggregated.T, delta, preferred_element_type=jnp.float32)
    bias_grad = lax.optimization_barrier(jnp.sum(delta.astype(jnp.float32), axis=0))
    back = jnp.dot(delta, weight.T, preferred_element_type=jnp.float32).astype(jnp.bfloat16)
    back_tiles = back.reshape(NODES // TILE, TILE, F)

    def backward_step(acc, item):
        tiles, rws, cls, live = item
        sources = back_tiles[rws]
        prod = jnp.einsum('sik,sif->skf', tiles.astype(jnp.float32), sources.astype(jnp.float32))
        prod = prod * live[:, None, None]
        return (acc.at[cls].add(prod), None)
    start_back = jnp.zeros((NODES // TILE, TILE, F), jnp.float32)
    total_back, _ = lax.scan(backward_step, start_back, (values, row_tiles, col_tiles, alive))
    feature_grad = total_back.reshape(NODES, F)
    return (activations, feature_grad, weight_grad, bias_grad)
```

```python
import functools

import jax
import jax.numpy as jnp
from jax import lax
from jax.experimental import pallas as pl
from jax.experimental.pallas import tpu as pltpu
from jax.sharding import Mesh, PartitionSpec as P

AXES = ("yl", "z", "c", "yh", "x")
SIZES = (2, 8, 2, 2, 4)
DOM = ("yl", "z", "c")
PEERS = ("yl", "z")
REP = ("yh", "x")

TILE = 128
SLOTS = 32
ROW_TILES = 8
NX = 4
NH = 2
NP = 16
WIDE = 128
THIN = WIDE // NX
MAIN = ROW_TILES * THIN
EXTRA = 32
CHUNK = MAIN + EXTRA
GRADS = WIDE // (NX * NH)
META = 3 * SLOTS
UNROLL = 16

F32 = jnp.float32
BF16 = jnp.bfloat16
CONTRACT_LAST = (((1,), (1,)), ((), ()))
CONTRACT_FIRST = (((0,), (0,)), ((), ()))
PLAIN = (((1,), (0,)), ((), ()))


def mul(a, b, how):
    return lax.dot_general(a, b, how, preferred_element_type=F32)


def params(mb):
    return pltpu.CompilerParams(vmem_limit_bytes=mb * 1024 * 1024)


def prep_kernel(ids, feat, out):
    first = ids[0] * THIN
    rows = lax.broadcasted_iota(jnp.int32, (THIN, WIDE), 0) + first
    cols = lax.broadcasted_iota(jnp.int32, (THIN, WIDE), 1)
    pick = (rows == cols).astype(BF16)
    for t in range(ROW_TILES):
        part = mul(pick, feat[t * TILE : (t + 1) * TILE, :], CONTRACT_LAST).astype(BF16)
        for p in range(NP):
            out[p, t * THIN : (t + 1) * THIN, :] = part


def slot_place(meta, at, s):
    row = meta[at + s]
    col = meta[at + SLOTS + s]
    live = s < meta[at + 2 * SLOTS]
    owner = col // ROW_TILES
    core = owner % 2
    place = (owner // 2) * ROW_TILES + col % ROW_TILES
    return row, core, place, live


def forward_kernel(ids, meta, tiles, mine, other, out, acc):
    i = pl.program_id(0)

    @pl.when(i == 0)
    def _():
        acc[...] = jnp.zeros_like(acc)

    at = ((ids[0] - i + NX) % NX) * META
    my_core = ids[1]

    def body(g, carry):
        rows, prods = [], []
        for u in range(UNROLL):
            s = g * UNROLL + u
            row, core, place, live = slot_place(meta, at, s)
            src = jnp.where(core == my_core, mine[place], other[place])
            src = jnp.where(live, src, jnp.zeros_like(src))
            prods.append(mul(src, tiles[0, s], CONTRACT_LAST))
            rows.append(row)
        for row, prod in zip(rows, prods):
            acc[row] += prod
        return carry

    lax.fori_loop(0, SLOTS // UNROLL, body, 0)

    @pl.when(i == NX - 1)
    def _():
        done = acc[...].astype(BF16)
        for r in range(NX * NH):
            out[r] = done


def backward_kernel(ids, meta, tiles, parts, weight, bias, cot, act, keep, send, acc, back):
    i = pl.program_id(0)

    @pl.when(i == 0)
    def _():
        acc[...] = jnp.zeros_like(acc)
        x_at = pl.multiple_of(ids[0] * THIN, THIN)
        r_at = pl.multiple_of(ids[2] * GRADS, GRADS)
        w_rows = weight[pl.ds(x_at, THIN), :]
        grow = lax.broadcasted_iota(jnp.int32, (GRADS, WIDE), 0) + r_at
        gcol = lax.broadcasted_iota(jnp.int32, (GRADS, WIDE), 1)
        gpick = (grow == gcol).astype(BF16)
        wsum = jnp.zeros((GRADS, WIDE), F32)
        bsum = jnp.zeros((1, WIDE), F32)
        for t in range(ROW_TILES):
            agg_t = jnp.concatenate(
                [parts[x, t].astype(F32) + parts[NX + x, t].astype(F32) for x in range(NX)], axis=0
            ).astype(BF16)
            pre = mul(agg_t, weight[...], CONTRACT_FIRST) + bias[...]
            sq = pre * pre
            th = jnp.tanh(0.7978845608028654 * pre * (1.0 + 0.044715 * sq))
            half = 0.5 * (1.0 + th)
            act[t * TILE : (t + 1) * TILE, :] = (pre * half).astype(BF16)
            slope = half + 0.5 * pre * (1.0 - th * th) * (
                0.7978845608028654 * (1.0 + (3 * 0.044715) * sq)
            )
            delta = (cot[t * TILE : (t + 1) * TILE, :].astype(F32) * slope).astype(BF16)
            back[t] = mul(w_rows, delta, CONTRACT_LAST).astype(BF16)
            own = mul(gpick, agg_t, PLAIN).astype(BF16)
            wsum = wsum + mul(own, delta, PLAIN)
            bsum = bsum + jnp.sum(delta.astype(F32), axis=0, keepdims=True)
        rest = jnp.where(
            lax.broadcasted_iota(jnp.int32, (EXTRA - GRADS, WIDE), 0) == 0,
            jnp.broadcast_to(bsum, (EXTRA - GRADS, WIDE)),
            0.0,
        )
        extra = jnp.concatenate([wsum, rest], axis=0).astype(BF16)
        for p in range(NP):
            keep[p, MAIN:, :] = extra
            send[p, MAIN:, :] = extra

    at = ((ids[0] - i + NX) % NX) * META
    my_core = ids[1]

    def body(g, carry):
        places, prods = [], []
        for u in range(UNROLL):
            s = g * UNROLL + u
            row, core, place, live = slot_place(meta, at, s)
            src = jnp.where(live, back[row], jnp.zeros((THIN, TILE), BF16))
            prods.append(mul(src, tiles[0, s], PLAIN))
            places.append(jnp.where(core == my_core, 0, NP * ROW_TILES) + place)
        for place, prod in zip(places, prods):
            acc[place] += prod
        return carry

    lax.fori_loop(0, SLOTS // UNROLL, body, 0)

    @pl.when(i == NX - 1)
    def _():
        for p in range(NP):
            for t in range(ROW_TILES):
                keep[p, t * THIN : (t + 1) * THIN, :] = acc[p * ROW_TILES + t].astype(BF16)
                send[p, t * THIN : (t + 1) * THIN, :] = acc[(NP + p) * ROW_TILES + t].astype(BF16)


def gather_sum_kernel(got, out):
    total = got[0].astype(F32)
    for p in range(1, NP):
        total = total + got[p].astype(F32)
    total = total.astype(BF16)
    for r in range(NX * NH):
        out[r] = total


def finish_kernel(got, grad, wgrad, bgrad):
    for t in range(ROW_TILES):
        rows = slice(t * THIN, (t + 1) * THIN)
        block = jnp.concatenate(
            [got[x, rows, :].astype(F32) + got[NX + x, rows, :].astype(F32) for x in range(NX)], axis=0
        )
        grad[t * TILE : (t + 1) * TILE, :] = block.T
    for r in range(NX * NH):
        wgrad[r * GRADS : (r + 1) * GRADS, :] = got[r, MAIN : MAIN + GRADS, :].astype(F32)
    bgrad[...] = got[0, MAIN + GRADS : CHUNK, :].astype(F32)[0:1, :]


def rotate(value, step):
    return lax.ppermute(value, "x", [(k, (k + step) % NX) for k in range(NX)])


def swap_core(value):
    return lax.ppermute(value, "c", [(0, 1), (1, 0)])


def exchange(value, axes):
    return lax.all_to_all(value, axes, 0, 0, tiled=True)


def whole(shape):
    return pl.BlockSpec(shape, lambda *_: (0,) * len(shape))


def shards(features, tile_values, tile_rows, tile_cols, tile_count, weight, bias, cotangent):
    x = lax.axis_index("x").astype(jnp.int32)
    core = lax.axis_index("c").astype(jnp.int32)
    r = lax.axis_index("yh").astype(jnp.int32) * NX + x
    ids = jnp.stack([x, core, r])
    tiles = lax.all_gather(tile_values[0, 0], "x", axis=0)
    own_meta = jnp.concatenate(
        [
            tile_rows[0, 0],
            tile_cols[0, 0],
            jnp.broadcast_to(tile_count[0, 0], (SLOTS,)),
        ]
    )
    meta = jnp.concatenate([own_meta] + [rotate(own_meta, k) for k in range(1, NX)])

    copies = pl.pallas_call(
        prep_kernel,
        out_shape=jax.ShapeDtypeStruct((NP, MAIN, TILE), BF16),
        grid_spec=pltpu.PrefetchScalarGridSpec(
            num_scalar_prefetch=1,
            grid=(1,),
            in_specs=[whole((ROW_TILES * TILE, WIDE))],
            out_specs=whole((NP, MAIN, TILE)),
        ),
        compiler_params=params(16),
        name="prep",
    )(ids, features)
    mine = exchange(copies, PEERS)
    other = swap_core(mine)
    mine = mine.reshape(NP * ROW_TILES, THIN, TILE)
    other = other.reshape(NP * ROW_TILES, THIN, TILE)

    tile_spec = pl.BlockSpec((1, SLOTS, TILE, TILE), lambda i, *_: (i, 0, 0, 0))
    parts = pl.pallas_call(
        forward_kernel,
        out_shape=jax.ShapeDtypeStruct((NX * NH, ROW_TILES, THIN, TILE), BF16),
        grid_spec=pltpu.PrefetchScalarGridSpec(
            num_scalar_prefetch=2,
            grid=(NX,),
            in_specs=[tile_spec, whole(mine.shape), whole(other.shape)],
            out_specs=whole((NX * NH, ROW_TILES, THIN, TILE)),
            scratch_shapes=[pltpu.VMEM((ROW_TILES, THIN, TILE), F32)],
        ),
        compiler_params=params(32),
        name="forward",
    )(ids, meta, tiles, mine, other)
    parts = exchange(parts, REP)

    activations, keep, send = pl.pallas_call(
        backward_kernel,
        out_shape=(
            jax.ShapeDtypeStruct((ROW_TILES * TILE, WIDE), BF16),
            jax.ShapeDtypeStruct((NP, CHUNK, TILE), BF16),
            jax.ShapeDtypeStruct((NP, CHUNK, TILE), BF16),
        ),
        grid_spec=pltpu.PrefetchScalarGridSpec(
            num_scalar_prefetch=2,
            grid=(NX,),
            in_specs=[
                tile_spec,
                whole(parts.shape),
                whole((WIDE, WIDE)),
                whole((1, WIDE)),
                whole((ROW_TILES * TILE, WIDE)),
            ],
            out_specs=(
                whole((ROW_TILES * TILE, WIDE)),
                whole((NP, CHUNK, TILE)),
                whole((NP, CHUNK, TILE)),
            ),
            scratch_shapes=[
                pltpu.VMEM((2 * NP * ROW_TILES, THIN, TILE), F32),
                pltpu.VMEM((ROW_TILES, THIN, TILE), BF16),
            ],
        ),
        compiler_params=params(40),
        name="backward",
    )(ids, meta, tiles, parts, weight, bias.reshape(1, WIDE), cotangent)

    paired = (keep.astype(F32) + swap_core(send).astype(F32)).astype(BF16)
    got = exchange(paired, PEERS)
    shared = pl.pallas_call(
        gather_sum_kernel,
        out_shape=jax.ShapeDtypeStruct((NX * NH, CHUNK, TILE), BF16),
        compiler_params=params(16),
        name="gather_sum",
    )(got)
    got = exchange(shared, REP)
    feature_grad, weight_grad, bias_grad = pl.pallas_call(
        finish_kernel,
        out_shape=(
            jax.ShapeDtypeStruct((ROW_TILES * TILE, WIDE), F32),
            jax.ShapeDtypeStruct((WIDE, WIDE), F32),
            jax.ShapeDtypeStruct((1, WIDE), F32),
        ),
        compiler_params=params(16),
        name="finish",
    )(got)
    return (activations, feature_grad, weight_grad, bias_grad.reshape(WIDE))


def solution(mesh):
    fine = Mesh(mesh.devices.reshape(SIZES), AXES)
    return jax.shard_map(
        shards,
        mesh=fine,
        in_specs=(
            P(DOM, None),
            P(DOM, REP, None, None, None),
            P(DOM, REP, None),
            P(DOM, REP, None),
            P(DOM, REP),
            P(),
            P(),
            P(DOM, None),
        ),
        out_specs=(P(DOM, None), P(DOM, None), P(), P()),
        check_vma=False,
    )
```

```python
import jax
import jax.numpy as jnp
from jax import lax
from jax.experimental import pallas as pl
from jax.experimental.pallas import tpu as pltpu
from jax.sharding import Mesh, PartitionSpec as P

AXES = ("yl", "z", "c", "yh", "x")
SIZES = (2, 8, 2, 2, 4)
DOM = ("yl", "z", "c")
PEERS = ("yl", "z")
REP = ("yh", "x")

TILE = 128
SLOTS = 32
HALF = SLOTS // 2
ROW_TILES = 8
NX = 4
NY = 4
NZ = 8
NP = 16
NR = 8
WIDE = 128
THIN = WIDE // NX
MAIN = ROW_TILES * THIN
BLOCK_HALF = ROW_TILES // 2
LAST = BLOCK_HALF * THIN
GRADS = THIN // 2
EXTRA = 32
SWAPS = 4
PIECE = NZ * LAST
META = 128
RELAY_COST = pl.CostEstimate(flops=20 * 10**9, bytes_accessed=60 * 10**6, transcendentals=0)
UNROLL = 16

F32 = jnp.float32
BF16 = jnp.bfloat16
CONTRACT_LAST = (((1,), (1,)), ((), ()))
CONTRACT_FIRST = (((0,), (0,)), ((), ()))
PLAIN = (((1,), (0,)), ((), ()))


def mul(a, b, how):
    return lax.dot_general(a, b, how, preferred_element_type=F32)


def prep_kernel(ids, feat, out):
    first = ids[0] * THIN
    rows = lax.broadcasted_iota(jnp.int32, (THIN, WIDE), 0) + first
    cols = lax.broadcasted_iota(jnp.int32, (THIN, WIDE), 1)
    pick = (rows == cols).astype(BF16)
    for t in range(ROW_TILES):
        part = mul(pick, feat[t * TILE : (t + 1) * TILE, :], CONTRACT_LAST).astype(BF16)
        for p in range(NP):
            out[p, t * THIN : (t + 1) * THIN, :] = part


def each_group(tile_refs, work):
    for ref, source, skip in tile_refs:
        lax.fori_loop(
            0, ref.shape[0] // UNROLL, lambda g, _, a=ref, b=source, c=skip: work(a, b, c, g), 0
        )


def relay_kernel(left, right, own_meta, meta_l, meta_r, meta_f, out_a, out_b, meta):
    out_a[...] = left[0:HALF]
    out_b[...] = right[HALF:SLOTS]
    for k, part in enumerate((own_meta, meta_l, meta_r, meta_f)):
        meta[k : k + 1, :] = part[...]


def forward_kernel(ids, meta, own, left, right, far_a, far_b, mine, *rest):
    others, out = rest[:SWAPS], rest[SWAPS]
    out[...] = jnp.zeros_like(out)
    my_core = ids[1]
    per = NP * ROW_TILES // SWAPS

    def work(tiles, source, skip, g):
        at = source * META
        rows, prods = [], []
        for u in range(UNROLL):
            s = g * UNROLL + u
            row = meta[at + skip + s]
            col = meta[at + SLOTS + skip + s]
            live = skip + s < meta[at + 2 * SLOTS]
            owner = col // ROW_TILES
            place = (owner // 2) * ROW_TILES + col % ROW_TILES
            src, inner = mine[place], place % per
            for k, other in enumerate(others):
                here = (owner % 2 != my_core) & (place // per == k)
                src = jnp.where(here, other[inner], src)
            src = jnp.where(live, src, jnp.zeros_like(src))
            prods.append(mul(src, tiles[s], CONTRACT_LAST))
            rows.append(row)
        for row, prod in zip(rows, prods):
            out[row] += prod
        return 0

    each_group([(own, 0, 0), (left, 1, 0), (right, 2, 0), (far_a, 3, 0), (far_b, 3, HALF)], work)


def backward_kernel(
    ids, meta, own, left, right, far_a, far_b, agg, agg_l, agg_r, agg_f, weight, bias, cot,
    act, keep, send, acc, back, full, slopes, wsum,
):
    x, my_core, yl, yh = ids[0], ids[1], ids[2], ids[3]
    acc[...] = jnp.zeros_like(acc)
    for t in range(ROW_TILES):
        for k, part in ((0, agg), (1, agg_l), (3, agg_r), (2, agg_f)):
            full[t, pl.ds(pl.multiple_of(((x - k + NX) % NX) * THIN, THIN), THIN), :] = part[t]
    w_rows = weight[pl.ds(pl.multiple_of(x * THIN, THIN), THIN), :]
    for t in range(ROW_TILES):
        pre = mul(full[t], weight[...], CONTRACT_FIRST) + bias[...]
        sq = pre * pre
        th = jnp.tanh(0.7978845608028654 * pre * (1.0 + 0.044715 * sq))
        half = 0.5 * (1.0 + th)
        act[t * TILE : (t + 1) * TILE, :] = (pre * half).astype(BF16)
        slope = half + 0.5 * pre * (1.0 - th * th) * (
            0.7978845608028654 * (1.0 + (3 * 0.044715) * sq)
        )
        delta = (cot[t * TILE : (t + 1) * TILE, :].astype(F32) * slope).astype(BF16)
        slopes[t] = delta
        back[t] = mul(w_rows, delta, CONTRACT_LAST).astype(BF16)
    bsum = jnp.zeros((1, WIDE), F32)
    wpart = jnp.zeros((THIN, WIDE), F32)
    for t in range(BLOCK_HALF):
        at = yh * BLOCK_HALF + t
        delta = slopes[at]
        wpart = wpart + mul(agg[at], delta, PLAIN)
        bsum = bsum + jnp.sum(delta.astype(F32), axis=0, keepdims=True)
    wsum[...] = wpart
    rest = jnp.where(
        lax.broadcasted_iota(jnp.int32, (EXTRA - GRADS, WIDE), 0) == 0,
        jnp.broadcast_to(bsum, (EXTRA - GRADS, WIDE)),
        0.0,
    )
    y = yh * 2 + yl
    for k in range(NY):
        there = ((y + k) % NY) // 2
        some = wsum[pl.ds(pl.multiple_of(there * GRADS, GRADS), GRADS), :]
        extra = jnp.concatenate([some, rest], axis=0).astype(BF16)
        keep[k, PIECE:, :] = extra
        send[k, PIECE:, :] = extra

    def work(tiles, source, skip, g):
        at = source * META
        places, prods = [], []
        for u in range(UNROLL):
            s = g * UNROLL + u
            row = meta[at + skip + s]
            col = meta[at + SLOTS + skip + s]
            live = skip + s < meta[at + 2 * SLOTS]
            owner, block = col // ROW_TILES, col % ROW_TILES
            core, z, to_yl = owner % 2, (owner // 2) % NZ, owner // (2 * NZ)
            k = ((block // BLOCK_HALF) * 2 + to_yl - y + NY) % NY
            place = jnp.where(core == my_core, 0, NY) + k
            place = (place * NZ + z) * BLOCK_HALF + block % BLOCK_HALF
            src = jnp.where(live, back[row], jnp.zeros((THIN, TILE), BF16))
            prods.append(mul(src, tiles[s], PLAIN))
            places.append(place)
        for place, prod in zip(places, prods):
            acc[place] += prod
        return 0

    each_group([(own, 0, 0), (left, 1, 0), (right, 2, 0), (far_a, 3, 0), (far_b, 3, HALF)], work)
    per = NZ * BLOCK_HALF
    for k in range(NY):
        for i in range(per):
            keep[k, i * THIN : (i + 1) * THIN, :] = acc[k * per + i].astype(BF16)
            send[k, i * THIN : (i + 1) * THIN, :] = acc[(NY + k) * per + i].astype(BF16)


def pair_kernel(keep, got, *outs):
    for k, out in enumerate(outs):
        out[...] = (keep[k].astype(F32) + got[k].astype(F32)).astype(BF16)


def y_sum_kernel(own, before, across, after, out):
    def total(rows):
        near = own[rows, :].astype(F32) + across[rows, :].astype(F32)
        return (near + (before[rows, :].astype(F32) + after[rows, :].astype(F32))).astype(BF16)

    extra = total(slice(PIECE, PIECE + EXTRA))
    for z in range(NZ):
        out[z, 0:LAST, :] = total(slice(z * LAST, (z + 1) * LAST))
        out[z, LAST:, :] = extra


def z_sum_kernel(got, out):
    total = got[0].astype(F32)
    for z in range(1, NZ):
        total = total + got[z].astype(F32)
    total = total.astype(BF16)
    for r in range(NR):
        out[r] = total


def finish_kernel(got, grad, wgrad, bgrad):
    for t in range(ROW_TILES):
        first = (t // BLOCK_HALF) * NX
        at = (t % BLOCK_HALF) * THIN
        block = jnp.concatenate(
            [got[first + x, at : at + THIN, :].astype(F32) for x in range(NX)], axis=0
        )
        grad[t * TILE : (t + 1) * TILE, :] = block.T
    for yh in range(2):
        for x in range(NX):
            to = x * THIN + yh * GRADS
            wgrad[to : to + GRADS, :] = got[yh * NX + x, LAST : LAST + GRADS, :].astype(F32)
    bgrad[...] = got[0, LAST + GRADS : LAST + EXTRA, :].astype(F32)[0:1, :]


def rotate(value, step):
    return lax.ppermute(value, "x", [(k, (k + step) % NX) for k in range(NX)])


def along_y(value, step):
    pairs = []
    for y in range(NY):
        to = (y + step) % NY
        pairs.append(((y % 2) * 2 + y // 2, (to % 2) * 2 + to // 2))
    return lax.ppermute(value, ("yl", "yh"), pairs)


def swap(value, axis):
    return lax.ppermute(value, axis, [(0, 1), (1, 0)])


def exchange(value, axes):
    return lax.all_to_all(value, axes, 0, 0, tiled=True)


def kernel_call(body, name, outs, scalars, scratch, mb, *args, cost=None):
    one = isinstance(outs, tuple)
    shapes = [outs] if one else outs
    result = pl.pallas_call(
        body,
        out_shape=[jax.ShapeDtypeStruct(s, d) for s, d in shapes],
        grid_spec=pltpu.PrefetchScalarGridSpec(
            num_scalar_prefetch=scalars,
            grid=(),
            in_specs=[pl.BlockSpec(memory_space=pltpu.VMEM)] * (len(args) - scalars),
            out_specs=[pl.BlockSpec(memory_space=pltpu.VMEM)] * len(shapes),
            scratch_shapes=scratch,
        ),
        compiler_params=pltpu.CompilerParams(vmem_limit_bytes=mb * 1024 * 1024),
        cost_estimate=cost,
        name=name,
    )(*args)
    return result[0] if one else result


def shards(features, tile_values, tile_rows, tile_cols, tile_count, weight, bias, cotangent):
    x, core, yl, yh = (lax.axis_index(a).astype(jnp.int32) for a in ("x", "c", "yl", "yh"))
    ids = jnp.stack([x, core, yl, yh])
    own = tile_values[0, 0]
    left = rotate(own, 1)
    right = rotate(own, NX - 1)
    count = jnp.broadcast_to(tile_count, (1, META - 2 * SLOTS))
    own_meta = jnp.concatenate([tile_rows[0], tile_cols[0], count], axis=1)
    half = ((HALF, TILE, TILE), BF16)
    pass_a, pass_b, meta = kernel_call(
        relay_kernel,
        "relay",
        [half, half, ((NX, META), jnp.int32)],
        0,
        [],
        16,
        left,
        right,
        own_meta,
        rotate(own_meta, 1),
        rotate(own_meta, NX - 1),
        rotate(own_meta, 2),
        cost=RELAY_COST,
    )
    meta = meta.reshape(NX * META)
    far_a, far_b = rotate(pass_a, 1), rotate(pass_b, NX - 1)
    tiles = (own, left, right, far_a, far_b)

    copies = kernel_call(prep_kernel, "prep", ((NP, MAIN, TILE), BF16), 1, [], 16, ids, features)
    mine = exchange(copies, PEERS)
    mine = mine.reshape(NP * ROW_TILES, THIN, TILE)
    per = NP * ROW_TILES // SWAPS
    others = [swap(mine[k * per : (k + 1) * per], "c") for k in range(SWAPS)]

    thin = (ROW_TILES, THIN, TILE)
    part = kernel_call(
        forward_kernel, "forward", (thin, F32), 2, [], 40, ids, meta, *tiles, mine, *others
    )
    agg = (part + swap(part, "yh")).astype(BF16)
    agg_l, agg_r, agg_f = rotate(agg, 1), rotate(agg, NX - 1), rotate(agg, 2)

    piece = PIECE + EXTRA
    square = (ROW_TILES, TILE, WIDE)
    activations, keep, send = kernel_call(
        backward_kernel,
        "backward",
        [((ROW_TILES * TILE, WIDE), BF16), ((NY, piece, TILE), BF16), ((NY, piece, TILE), BF16)],
        2,
        [
            pltpu.VMEM((2 * NY * NZ * BLOCK_HALF, THIN, TILE), F32),
            pltpu.VMEM(thin, BF16),
            pltpu.VMEM(square, BF16),
            pltpu.VMEM(square, BF16),
            pltpu.VMEM((THIN, WIDE), F32),
        ],
        40,
        ids,
        meta,
        *tiles,
        agg,
        agg_l,
        agg_r,
        agg_f,
        weight,
        bias.reshape(1, WIDE),
        cotangent,
    )
    got = swap(send, "c")
    stay, one, two, three = kernel_call(
        pair_kernel, "pair", [((piece, TILE), BF16)] * NY, 0, [], 16, keep, got
    )
    before, across, after = along_y(one, 1), along_y(two, 2), along_y(three, 3)
    last = LAST + EXTRA
    summed = kernel_call(
        y_sum_kernel, "y_sum", ((NZ, last, TILE), BF16), 0, [], 16, stay, before, across, after
    )
    got = exchange(summed, "z")
    shared = kernel_call(z_sum_kernel, "z_sum", ((NR, last, TILE), BF16), 0, [], 16, got)
    got = exchange(shared, REP)
    feature_grad, weight_grad, bias_grad = kernel_call(
        finish_kernel,
        "finish",
        [((ROW_TILES * TILE, WIDE), F32), ((WIDE, WIDE), F32), ((1, WIDE), F32)],
        0,
        [],
        16,
        got,
    )
    return (activations, feature_grad, weight_grad, bias_grad.reshape(WIDE))


def solution(mesh):
    fine = Mesh(mesh.devices.reshape(SIZES), AXES)
    return jax.shard_map(
        shards,
        mesh=fine,
        in_specs=(
            P(DOM, None),
            P(DOM, REP, None, None, None),
            P(DOM, REP, None),
            P(DOM, REP, None),
            P(DOM, REP),
            P(),
            P(),
            P(DOM, None),
        ),
        out_specs=(P(DOM, None), P(DOM, None), P(), P()),
        check_vma=False,
    )
```

```python
import jax
import jax.numpy as jnp
from jax import lax
from jax.experimental import pallas as pl
from jax.experimental.pallas import tpu as pltpu
from jax.sharding import Mesh, PartitionSpec as P

AXES = ("yl", "z", "c", "yh", "x")
SIZES = (2, 8, 2, 2, 4)
DOM = ("yl", "z", "c")
PEERS = ("yl", "z")
REP = ("yh", "x")

TILE = 128
SLOTS = 32
HALF = SLOTS // 2
ROW_TILES = 8
NX = 4
NY = 4
NZ = 8
NP = 16
NR = 8
WIDE = 128
THIN = WIDE // NX
MAIN = ROW_TILES * THIN
BLOCK_HALF = ROW_TILES // 2
LAST = BLOCK_HALF * THIN
GRADS = THIN // 2
EXTRA = 32
SWAPS = 2
PIECE = NZ * LAST
META = 4 * SLOTS
RELAY_COST = pl.CostEstimate(flops=14 * 10**9, bytes_accessed=42 * 10**6, transcendentals=0)
UNROLL = 16

F32 = jnp.float32
BF16 = jnp.bfloat16
CONTRACT_LAST = (((1,), (1,)), ((), ()))
CONTRACT_FIRST = (((0,), (0,)), ((), ()))
PLAIN = (((1,), (0,)), ((), ()))


def mul(a, b, how):
    return lax.dot_general(a, b, how, preferred_element_type=F32)


def prep_kernel(ids, feat, out):
    first = ids[0] * THIN
    rows = lax.broadcasted_iota(jnp.int32, (THIN, WIDE), 0) + first
    cols = lax.broadcasted_iota(jnp.int32, (THIN, WIDE), 1)
    pick = (rows == cols).astype(BF16)
    for t in range(ROW_TILES):
        part = mul(pick, feat[t * TILE : (t + 1) * TILE, :], CONTRACT_LAST).astype(BF16)
        for p in range(NP):
            out[p, t * THIN : (t + 1) * THIN, :] = part


def every_slot(tile_refs, work):
    for ref, meta, skip in tile_refs:
        prods = [work(ref[s], meta, skip + s) for s in range(ref.shape[0])]
        for target, index, prod in prods:
            target[index] += prod


def relay_kernel(left, right, meta_l, meta_r, meta_f, out_a, out_b, out_l, out_r, out_f):
    out_a[...] = left[0:HALF]
    out_b[...] = right[HALF:SLOTS]
    out_l[...] = meta_l[...]
    out_r[...] = meta_r[...]
    out_f[...] = meta_f[...]


def forward_kernel(meta, meta_l, meta_r, meta_f, own, left, right, far_a, far_b, mine, *rest):
    others, (out, table, acc) = rest[:SWAPS], rest[SWAPS:]
    acc[...] = jnp.zeros_like(acc)
    half = NP * ROW_TILES
    table[0:half] = mine[...]
    for k, other in enumerate(others):
        per = half // SWAPS
        table[half + k * per : half + (k + 1) * per] = other[...]
    table[2 * half] = jnp.zeros((THIN, TILE), BF16)

    def work(tile, meta, s):
        return acc, meta[s], mul(tile, table[meta[SLOTS + s]], CONTRACT_LAST)

    groups = [(own, meta, 0), (left, meta_l, 0), (right, meta_r, 0), (far_a, meta_f, 0)]
    every_slot(groups + [(far_b, meta_f, HALF)], work)
    for t in range(ROW_TILES):
        out[t] = acc[t].T


def backward_kernel(
    ids, meta, meta_l, meta_r, meta_f, own, left, right, far_a, far_b, agg, agg_l, agg_r, agg_f, weight, bias, cot,
    act, keep, *rest,
):
    send, acc, back, full, slopes, wsum = rest
    x, yl, yh = ids[0], ids[2], ids[3]
    acc[...] = jnp.zeros_like(acc)
    for t in range(ROW_TILES):
        for k, part in ((0, agg), (1, agg_l), (3, agg_r), (2, agg_f)):
            full[t, pl.ds(pl.multiple_of(((x - k + NX) % NX) * THIN, THIN), THIN), :] = part[t]
    w_rows = weight[pl.ds(pl.multiple_of(x * THIN, THIN), THIN), :]
    for t in range(ROW_TILES):
        pre = mul(full[t], weight[...], CONTRACT_FIRST) + bias[...]
        sq = pre * pre
        th = jnp.tanh(0.7978845608028654 * pre * (1.0 + 0.044715 * sq))
        half = 0.5 * (1.0 + th)
        act[t * TILE : (t + 1) * TILE, :] = (pre * half).astype(BF16)
        slope = half + 0.5 * pre * (1.0 - th * th) * (
            0.7978845608028654 * (1.0 + (3 * 0.044715) * sq)
        )
        delta = (cot[t * TILE : (t + 1) * TILE, :].astype(F32) * slope).astype(BF16)
        slopes[t] = delta
        back[t] = mul(w_rows, delta, CONTRACT_LAST).astype(BF16)
    bsum = jnp.zeros((1, WIDE), F32)
    wpart = jnp.zeros((THIN, WIDE), F32)
    for t in range(BLOCK_HALF):
        at = yh * BLOCK_HALF + t
        delta = slopes[at]
        wpart = wpart + mul(agg[at], delta, PLAIN)
        bsum = bsum + jnp.sum(delta.astype(F32), axis=0, keepdims=True)
    wsum[...] = wpart
    rest = jnp.where(
        lax.broadcasted_iota(jnp.int32, (EXTRA - GRADS, WIDE), 0) == 0,
        jnp.broadcast_to(bsum, (EXTRA - GRADS, WIDE)),
        0.0,
    )
    y = yh * 2 + yl
    for k in range(NY):
        there = ((y + k) % NY) // 2
        some = wsum[pl.ds(pl.multiple_of(there * GRADS, GRADS), GRADS), :]
        extra = jnp.concatenate([some, rest], axis=0).astype(BF16)
        keep[k, PIECE:, :] = extra
        send[k, PIECE:, :] = extra

    back[ROW_TILES] = jnp.zeros((THIN, TILE), BF16)

    def work(tile, meta, s):
        return acc, meta[3 * SLOTS + s], mul(back[meta[2 * SLOTS + s]], tile, PLAIN)

    groups = [(own, meta, 0), (left, meta_l, 0), (right, meta_r, 0), (far_a, meta_f, 0)]
    every_slot(groups + [(far_b, meta_f, HALF)], work)
    per = NZ * BLOCK_HALF
    for k in range(NY):
        for i in range(per):
            keep[k, i * THIN : (i + 1) * THIN, :] = acc[k * per + i].astype(BF16)
            send[k, i * THIN : (i + 1) * THIN, :] = acc[(NY + k) * per + i].astype(BF16)


def pair_kernel(keep, got, *outs):
    for k, out in enumerate(outs):
        out[...] = (keep[k].astype(F32) + got[k].astype(F32)).astype(BF16)


def y_sum_kernel(own, before, across, after, out):
    def total(rows):
        near = own[rows, :].astype(F32) + across[rows, :].astype(F32)
        return (near + (before[rows, :].astype(F32) + after[rows, :].astype(F32))).astype(BF16)

    extra = total(slice(PIECE, PIECE + EXTRA))
    for z in range(NZ):
        out[z, 0:LAST, :] = total(slice(z * LAST, (z + 1) * LAST))
        out[z, LAST:, :] = extra


def z_sum_kernel(got, out):
    total = got[0].astype(F32)
    for z in range(1, NZ):
        total = total + got[z].astype(F32)
    total = total.astype(BF16)
    for r in range(NR):
        out[r] = total


def finish_kernel(got, grad, wgrad, bgrad):
    for t in range(ROW_TILES):
        first = (t // BLOCK_HALF) * NX
        at = (t % BLOCK_HALF) * THIN
        block = jnp.concatenate(
            [got[first + x, at : at + THIN, :].astype(F32) for x in range(NX)], axis=0
        )
        grad[t * TILE : (t + 1) * TILE, :] = block.T
    for yh in range(2):
        for x in range(NX):
            to = x * THIN + yh * GRADS
            wgrad[to : to + GRADS, :] = got[yh * NX + x, LAST : LAST + GRADS, :].astype(F32)
    bgrad[...] = got[0, LAST + GRADS : LAST + EXTRA, :].astype(F32)[0:1, :]


def slot_meta(rows, cols, count, core, y):
    live = lax.broadcasted_iota(jnp.int32, rows.shape, 1) < count
    owner, block = cols // ROW_TILES, cols % ROW_TILES
    apart = jnp.where(owner % 2 == core, 0, 1)
    peer = owner // 2
    source = (apart * NP + peer) * ROW_TILES + block
    step = ((block // BLOCK_HALF) * 2 + peer // NZ - y + NY) % NY
    target = ((apart * NY + step) * NZ + peer % NZ) * BLOCK_HALF + block % BLOCK_HALF
    return jnp.concatenate(
        [
            rows,
            jnp.where(live, source, 2 * NP * ROW_TILES),
            jnp.where(live, rows, ROW_TILES),
            target,
        ],
        axis=1,
    )


def rotate(value, step):
    return lax.ppermute(value, "x", [(k, (k + step) % NX) for k in range(NX)])


def along_y(value, step):
    pairs = []
    for y in range(NY):
        to = (y + step) % NY
        pairs.append(((y % 2) * 2 + y // 2, (to % 2) * 2 + to // 2))
    return lax.ppermute(value, ("yl", "yh"), pairs)


def swap(value, axis):
    return lax.ppermute(value, axis, [(0, 1), (1, 0)])


def exchange(value, axes):
    return lax.all_to_all(value, axes, 0, 0, tiled=True)


def kernel_call(body, name, outs, scalars, scratch, mb, *args, cost=None):
    one = isinstance(outs, tuple)
    shapes = [outs] if one else outs
    result = pl.pallas_call(
        body,
        out_shape=[jax.ShapeDtypeStruct(s, d) for s, d in shapes],
        grid_spec=pltpu.PrefetchScalarGridSpec(
            num_scalar_prefetch=scalars,
            grid=(),
            in_specs=[pl.BlockSpec(memory_space=pltpu.VMEM)] * (len(args) - scalars),
            out_specs=[pl.BlockSpec(memory_space=pltpu.VMEM)] * len(shapes),
            scratch_shapes=scratch,
        ),
        compiler_params=pltpu.CompilerParams(vmem_limit_bytes=mb * 1024 * 1024),
        cost_estimate=cost,
        name=name,
    )(*args)
    return result[0] if one else result


def shards(features, tile_values, tile_rows, tile_cols, tile_count, weight, bias, cotangent):
    x, core, yl, yh = (lax.axis_index(a).astype(jnp.int32) for a in ("x", "c", "yl", "yh"))
    ids = jnp.stack([x, core, yl, yh])
    own = tile_values[0, 0]
    left = rotate(own, 1)
    right = rotate(own, NX - 1)
    own_meta = slot_meta(tile_rows[0], tile_cols[0], tile_count, core, yh * 2 + yl)
    half = ((HALF, TILE, TILE), BF16)
    line = ((1, META), jnp.int32)
    pass_a, pass_b, *metas = kernel_call(
        relay_kernel,
        "relay",
        [half, half, line, line, line],
        0,
        [],
        6,
        left,
        right,
        rotate(own_meta, 1),
        rotate(own_meta, NX - 1),
        rotate(own_meta, 2),
        cost=RELAY_COST,
    )
    metas = [m.reshape(META) for m in (own_meta, *metas)]
    far_a, far_b = rotate(pass_a, 1), rotate(pass_b, NX - 1)
    tiles = (own, left, right, far_a, far_b)

    copies = kernel_call(prep_kernel, "prep", ((NP, MAIN, TILE), BF16), 1, [], 6, ids, features)
    mine = exchange(copies, PEERS)
    mine = mine.reshape(NP * ROW_TILES, THIN, TILE)
    per = NP * ROW_TILES // SWAPS
    others = [swap(mine[k * per : (k + 1) * per], "c") for k in range(SWAPS)]

    thin = (ROW_TILES, THIN, TILE)
    scratch = [
        pltpu.VMEM((2 * NP * ROW_TILES + 1, THIN, TILE), BF16),
        pltpu.VMEM((ROW_TILES, TILE, THIN), F32),
    ]
    part = kernel_call(
        forward_kernel, "forward", (thin, F32), 4, scratch, 16, *metas, *tiles, mine, *others
    )
    agg = (part + swap(part, "yh")).astype(BF16)
    agg_l, agg_r, agg_f = rotate(agg, 1), rotate(agg, NX - 1), rotate(agg, 2)

    piece = PIECE + EXTRA
    square = (ROW_TILES, TILE, WIDE)
    activations, keep, send = kernel_call(
        backward_kernel,
        "backward",
        [((ROW_TILES * TILE, WIDE), BF16), ((NY, piece, TILE), BF16), ((NY, piece, TILE), BF16)],
        5,
        [
            pltpu.VMEM((2 * NY * NZ * BLOCK_HALF, THIN, TILE), F32),
            pltpu.VMEM((ROW_TILES + 1, THIN, TILE), BF16),
            pltpu.VMEM(square, BF16),
            pltpu.VMEM(square, BF16),
            pltpu.VMEM((THIN, WIDE), F32),
        ],
        20,
        ids,
        *metas,
        *tiles,
        agg,
        agg_l,
        agg_r,
        agg_f,
        weight,
        bias.reshape(1, WIDE),
        cotangent,
    )
    got = swap(send, "c")
    stay, one, two, three = kernel_call(
        pair_kernel, "pair", [((piece, TILE), BF16)] * NY, 0, [], 12, keep, got
    )
    before, across, after = along_y(one, 1), along_y(two, 2), along_y(three, 3)
    last = LAST + EXTRA
    summed = kernel_call(
        y_sum_kernel, "y_sum", ((NZ, last, TILE), BF16), 0, [], 12, stay, before, across, after
    )
    got = exchange(summed, "z")
    shared = kernel_call(z_sum_kernel, "z_sum", ((NR, last, TILE), BF16), 0, [], 16, got)
    got = exchange(shared, REP)
    feature_grad, weight_grad, bias_grad = kernel_call(
        finish_kernel,
        "finish",
        [((ROW_TILES * TILE, WIDE), F32), ((WIDE, WIDE), F32), ((1, WIDE), F32)],
        0,
        [],
        16,
        got,
    )
    return (activations, feature_grad, weight_grad, bias_grad.reshape(WIDE))


def solution(mesh):
    fine = Mesh(mesh.devices.reshape(SIZES), AXES)
    return jax.shard_map(
        shards,
        mesh=fine,
        in_specs=(
            P(DOM, None),
            P(DOM, REP, None, None, None),
            P(DOM, REP, None),
            P(DOM, REP, None),
            P(DOM, REP),
            P(),
            P(),
            P(DOM, None),
        ),
        out_specs=(P(DOM, None), P(DOM, None), P(), P()),
        check_vma=False,
    )
```

```python
import functools

import jax
import jax.numpy as jnp
from jax import lax
from jax.experimental import pallas as pl
from jax.experimental.pallas import tpu as pltpu
from jax.sharding import Mesh, PartitionSpec as P

AXES = ("yl", "z", "c", "yh", "x")
SIZES = (2, 8, 2, 2, 4)
DOM = ("yl", "z", "c")
PEERS = ("yl", "z")
REP = ("yh", "x")

TILE = 128
SLOTS = 32
HALF = SLOTS // 2
ROW_TILES = 8
NX = 4
NY = 4
NZ = 8
NP = 16
NR = 8
WIDE = 128
THIN = WIDE // NX
MAIN = ROW_TILES * THIN
BLOCK_HALF = ROW_TILES // 2
LAST = BLOCK_HALF * THIN
GRADS = THIN // 2
EXTRA = 32
SWAPS = 2
PIECE = NZ * LAST
META = 4 * SLOTS
RELAY_COST = pl.CostEstimate(flops=14 * 10**9, bytes_accessed=42 * 10**6, transcendentals=0)
UNROLL = 16

F32 = jnp.float32
BF16 = jnp.bfloat16
CONTRACT_LAST = (((1,), (1,)), ((), ()))
CONTRACT_FIRST = (((0,), (0,)), ((), ()))
PLAIN = (((1,), (0,)), ((), ()))


def mul(a, b, how):
    return lax.dot_general(a, b, how, preferred_element_type=F32)


def prep_kernel(ids, feat, out):
    first = ids[0] * THIN
    rows = lax.broadcasted_iota(jnp.int32, (THIN, WIDE), 0) + first
    cols = lax.broadcasted_iota(jnp.int32, (THIN, WIDE), 1)
    pick = (rows == cols).astype(BF16)
    for t in range(ROW_TILES):
        part = mul(pick, feat[t * TILE : (t + 1) * TILE, :], CONTRACT_LAST).astype(BF16)
        for p in range(NP):
            out[p, t * THIN : (t + 1) * THIN, :] = part


def every_slot(tile_refs, work):
    for ref, meta, skip in tile_refs:
        prods = [work(ref[s], meta, skip + s) for s in range(ref.shape[0])]
        for target, index, prod in prods:
            target[index] += prod


def relay_kernel(left, right, meta_l, meta_r, meta_f, out_a, out_b, out_l, out_r, out_f):
    out_a[...] = left[0:HALF]
    out_b[...] = right[HALF:SLOTS]
    out_l[...] = meta_l[...]
    out_r[...] = meta_r[...]
    out_f[...] = meta_f[...]


def fetch_far(far_a, far_b, far, far_sem):
    copies = [
        pltpu.make_async_copy(ref, far.at[k], far_sem.at[k]) for k, ref in enumerate((far_a, far_b))
    ]
    for copy in copies:
        copy.start()
    return copies


def forward_kernel(meta, meta_l, meta_r, meta_f, own, left, right, far_a, far_b, mine, *rest):
    others, (out, table, acc, far, far_sem) = rest[:SWAPS], rest[SWAPS:]
    fetch = fetch_far(far_a, far_b, far, far_sem)
    acc[...] = jnp.zeros_like(acc)
    half = NP * ROW_TILES
    table[0:half] = mine[...]
    for k, other in enumerate(others):
        per = half // SWAPS
        table[half + k * per : half + (k + 1) * per] = other[...]
    table[2 * half] = jnp.zeros((THIN, TILE), BF16)

    def work(tile, meta, s):
        return acc, meta[s], mul(tile, table[meta[SLOTS + s]], CONTRACT_LAST)

    every_slot([(own, meta, 0), (left, meta_l, 0), (right, meta_r, 0)], work)
    for copy in fetch:
        copy.wait()
    every_slot([(far.at[0], meta_f, 0), (far.at[1], meta_f, HALF)], work)
    for t in range(ROW_TILES):
        out[t] = acc[t].T


def backward_kernel(
    ids, meta, meta_l, meta_r, meta_f, own, left, right, far_a, far_b, agg, agg_l, agg_r, agg_f, weight, bias, cot,
    act, keep, *rest,
):
    send_a, send_b, acc, back, full, slopes, wsum, far, act_in, far_sem, act_sem = rest
    sends = {1: send_a.at[0], 2: send_a.at[1], 3: send_b.at[0], 0: send_b.at[1]}
    fetch = fetch_far(far_a, far_b, far, far_sem)
    x, yl, yh = ids[0], ids[2], ids[3]
    acc[...] = jnp.zeros_like(acc)
    for t in range(ROW_TILES):
        for k, part in ((0, agg), (1, agg_l), (3, agg_r), (2, agg_f)):
            full[t, pl.ds(pl.multiple_of(((x - k + NX) % NX) * THIN, THIN), THIN), :] = part[t]
    w_rows = weight[pl.ds(pl.multiple_of(x * THIN, THIN), THIN), :]
    for t in range(ROW_TILES):
        pre = mul(full[t], weight[...], CONTRACT_FIRST) + bias[...]
        sq = pre * pre
        th = jnp.tanh(0.7978845608028654 * pre * (1.0 + 0.044715 * sq))
        half = 0.5 * (1.0 + th)
        act_in[t * TILE : (t + 1) * TILE, :] = (pre * half).astype(BF16)
        slope = half + 0.5 * pre * (1.0 - th * th) * (
            0.7978845608028654 * (1.0 + (3 * 0.044715) * sq)
        )
        delta = (cot[t * TILE : (t + 1) * TILE, :].astype(F32) * slope).astype(BF16)
        slopes[t] = delta
        back[t] = mul(w_rows, delta, CONTRACT_LAST).astype(BF16)
    give = pltpu.make_async_copy(act_in, act, act_sem)
    give.start()
    bsum = jnp.zeros((1, WIDE), F32)
    wpart = jnp.zeros((THIN, WIDE), F32)
    for t in range(BLOCK_HALF):
        at = yh * BLOCK_HALF + t
        delta = slopes[at]
        wpart = wpart + mul(agg[at], delta, PLAIN)
        bsum = bsum + jnp.sum(delta.astype(F32), axis=0, keepdims=True)
    wsum[...] = wpart
    rest = jnp.where(
        lax.broadcasted_iota(jnp.int32, (EXTRA - GRADS, WIDE), 0) == 0,
        jnp.broadcast_to(bsum, (EXTRA - GRADS, WIDE)),
        0.0,
    )
    y = yh * 2 + yl
    for k in range(NY):
        there = ((y + k) % NY) // 2
        some = wsum[pl.ds(pl.multiple_of(there * GRADS, GRADS), GRADS), :]
        extra = jnp.concatenate([some, rest], axis=0).astype(BF16)
        keep[k, PIECE:, :] = extra
        sends[k][PIECE:, :] = extra

    back[ROW_TILES] = jnp.zeros((THIN, TILE), BF16)

    def work(tile, meta, s):
        return acc, meta[3 * SLOTS + s], mul(back[meta[2 * SLOTS + s]], tile, PLAIN)

    every_slot([(own, meta, 0), (left, meta_l, 0), (right, meta_r, 0)], work)
    for copy in fetch:
        copy.wait()
    every_slot([(far.at[0], meta_f, 0), (far.at[1], meta_f, HALF)], work)
    per = NZ * BLOCK_HALF
    for k in range(NY):
        for i in range(per):
            keep[k, i * THIN : (i + 1) * THIN, :] = acc[k * per + i].astype(BF16)
            sends[k][i * THIN : (i + 1) * THIN, :] = acc[(NY + k) * per + i].astype(BF16)
    give.wait()


def pair_kernel(which, keep, got, *outs):
    for at, (k, out) in enumerate(zip(which, outs)):
        out[...] = (keep[k].astype(F32) + got[at].astype(F32)).astype(BF16)


def y_sum_kernel(own, before, across, after, out):
    def total(rows):
        near = own[rows, :].astype(F32) + across[rows, :].astype(F32)
        return (near + (before[rows, :].astype(F32) + after[rows, :].astype(F32))).astype(BF16)

    extra = total(slice(PIECE, PIECE + EXTRA))
    for z in range(NZ):
        out[z, 0:LAST, :] = total(slice(z * LAST, (z + 1) * LAST))
        out[z, LAST:, :] = extra


def z_sum_kernel(got, out):
    total = got[0].astype(F32)
    for z in range(1, NZ):
        total = total + got[z].astype(F32)
    total = total.astype(BF16)
    for r in range(NR):
        out[r] = total


def finish_kernel(got, grad, wgrad, bgrad):
    for t in range(ROW_TILES):
        first = (t // BLOCK_HALF) * NX
        at = (t % BLOCK_HALF) * THIN
        block = jnp.concatenate(
            [got[first + x, at : at + THIN, :].astype(F32) for x in range(NX)], axis=0
        )
        grad[t * TILE : (t + 1) * TILE, :] = block.T
    for yh in range(2):
        for x in range(NX):
            to = x * THIN + yh * GRADS
            wgrad[to : to + GRADS, :] = got[yh * NX + x, LAST : LAST + GRADS, :].astype(F32)
    bgrad[...] = got[0, LAST + GRADS : LAST + EXTRA, :].astype(F32)[0:1, :]


def slot_meta(rows, cols, count, core, y):
    live = lax.broadcasted_iota(jnp.int32, rows.shape, 1) < count
    owner, block = cols // ROW_TILES, cols % ROW_TILES
    apart = jnp.where(owner % 2 == core, 0, 1)
    peer = owner // 2
    source = (apart * NP + peer) * ROW_TILES + block
    step = ((block // BLOCK_HALF) * 2 + peer // NZ - y + NY) % NY
    target = ((apart * NY + step) * NZ + peer % NZ) * BLOCK_HALF + block % BLOCK_HALF
    return jnp.concatenate(
        [
            rows,
            jnp.where(live, source, 2 * NP * ROW_TILES),
            jnp.where(live, rows, ROW_TILES),
            target,
        ],
        axis=1,
    )


def rotate(value, step):
    return lax.ppermute(value, "x", [(k, (k + step) % NX) for k in range(NX)])


def along_y(value, step):
    pairs = []
    for y in range(NY):
        to = (y + step) % NY
        pairs.append(((y % 2) * 2 + y // 2, (to % 2) * 2 + to // 2))
    return lax.ppermute(value, ("yl", "yh"), pairs)


def swap(value, axis):
    return lax.ppermute(value, axis, [(0, 1), (1, 0)])


def exchange(value, axes):
    return lax.all_to_all(value, axes, 0, 0, tiled=True)


def place(loose):
    return pl.BlockSpec(memory_space=pl.ANY if loose else pltpu.VMEM)


def kernel_call(body, name, outs, scalars, scratch, mb, *args, cost=None, loose_in=(), loose_out=()):
    one = isinstance(outs, tuple)
    shapes = [outs] if one else outs
    result = pl.pallas_call(
        body,
        out_shape=[jax.ShapeDtypeStruct(s, d) for s, d in shapes],
        grid_spec=pltpu.PrefetchScalarGridSpec(
            num_scalar_prefetch=scalars,
            grid=(),
            in_specs=[place(i in loose_in) for i in range(len(args) - scalars)],
            out_specs=[place(i in loose_out) for i in range(len(shapes))],
            scratch_shapes=scratch,
        ),
        compiler_params=pltpu.CompilerParams(vmem_limit_bytes=mb * 1024 * 1024),
        cost_estimate=cost,
        name=name,
    )(*args)
    return result[0] if one else result


def pair(which, keep, got):
    outs = [(got.shape[1:], BF16)] * 2
    return kernel_call(functools.partial(pair_kernel, which), "pair", outs, 0, [], 12, keep, got)


def shards(features, tile_values, tile_rows, tile_cols, tile_count, weight, bias, cotangent):
    x, core, yl, yh = (lax.axis_index(a).astype(jnp.int32) for a in ("x", "c", "yl", "yh"))
    ids = jnp.stack([x, core, yl, yh])
    own = tile_values[0, 0]
    left = rotate(own, 1)
    right = rotate(own, NX - 1)
    own_meta = slot_meta(tile_rows[0], tile_cols[0], tile_count, core, yh * 2 + yl)
    half = ((HALF, TILE, TILE), BF16)
    line = ((1, META), jnp.int32)
    pass_a, pass_b, *metas = kernel_call(
        relay_kernel,
        "relay",
        [half, half, line, line, line],
        0,
        [],
        6,
        left,
        right,
        rotate(own_meta, 1),
        rotate(own_meta, NX - 1),
        rotate(own_meta, 2),
        cost=RELAY_COST,
    )
    metas = [m.reshape(META) for m in (own_meta, *metas)]
    far_a, far_b = rotate(pass_a, 1), rotate(pass_b, NX - 1)
    tiles = (own, left, right, far_a, far_b)

    copies = kernel_call(prep_kernel, "prep", ((NP, MAIN, TILE), BF16), 1, [], 6, ids, features)
    mine = exchange(copies, PEERS)
    mine = mine.reshape(NP * ROW_TILES, THIN, TILE)
    per = NP * ROW_TILES // SWAPS
    others = [swap(mine[k * per : (k + 1) * per], "c") for k in range(SWAPS)]

    thin = (ROW_TILES, THIN, TILE)
    scratch = [
        pltpu.VMEM((2 * NP * ROW_TILES + 1, THIN, TILE), BF16),
        pltpu.VMEM((ROW_TILES, TILE, THIN), F32),
        pltpu.VMEM((2, HALF, TILE, TILE), BF16),
        pltpu.SemaphoreType.DMA((2,)),
    ]
    part = kernel_call(
        forward_kernel, "forward", (thin, F32), 4, scratch, 16, *metas, *tiles, mine, *others, loose_in=(3, 4)
    )
    agg = (part + swap(part, "yh")).astype(BF16)
    agg_l, agg_r, agg_f = rotate(agg, 1), rotate(agg, NX - 1), rotate(agg, 2)

    piece = PIECE + EXTRA
    square = (ROW_TILES, TILE, WIDE)
    activations, keep, send_a, send_b = kernel_call(
        backward_kernel,
        "backward",
        [((ROW_TILES * TILE, WIDE), BF16), ((NY, piece, TILE), BF16)] + [((2, piece, TILE), BF16)] * 2,
        5,
        [
            pltpu.VMEM((2 * NY * NZ * BLOCK_HALF, THIN, TILE), F32),
            pltpu.VMEM((ROW_TILES + 1, THIN, TILE), BF16),
            pltpu.VMEM(square, BF16),
            pltpu.VMEM(square, BF16),
            pltpu.VMEM((THIN, WIDE), F32),
            pltpu.VMEM((2, HALF, TILE, TILE), BF16),
            pltpu.VMEM((ROW_TILES * TILE, WIDE), BF16),
            pltpu.SemaphoreType.DMA((2,)),
            pltpu.SemaphoreType.DMA(()),
        ],
        20,
        ids,
        *metas,
        *tiles,
        agg,
        agg_l,
        agg_r,
        agg_f,
        weight,
        bias.reshape(1, WIDE),
        cotangent,
        loose_in=(3, 4),
        loose_out=(0,),
    )
    one, two = pair((1, 2), keep, swap(send_a, "c"))
    three, stay = pair((3, 0), keep, swap(send_b, "c"))
    before, across, after = along_y(one, 1), along_y(two, 2), along_y(three, 3)
    last = LAST + EXTRA
    summed = kernel_call(
        y_sum_kernel, "y_sum", ((NZ, last, TILE), BF16), 0, [], 12, stay, before, across, after
    )
    got = exchange(summed, "z")
    shared = kernel_call(z_sum_kernel, "z_sum", ((NR, last, TILE), BF16), 0, [], 16, got)
    got = exchange(shared, REP)
    feature_grad, weight_grad, bias_grad = kernel_call(
        finish_kernel,
        "finish",
        [((ROW_TILES * TILE, WIDE), F32), ((WIDE, WIDE), F32), ((1, WIDE), F32)],
        0,
        [],
        16,
        got,
    )
    return (activations, feature_grad, weight_grad, bias_grad.reshape(WIDE))


def solution(mesh):
    fine = Mesh(mesh.devices.reshape(SIZES), AXES)
    return jax.shard_map(
        shards,
        mesh=fine,
        in_specs=(
            P(DOM, None),
            P(DOM, REP, None, None, None),
            P(DOM, REP, None),
            P(DOM, REP, None),
            P(DOM, REP),
            P(),
            P(),
            P(DOM, None),
        ),
        out_specs=(P(DOM, None), P(DOM, None), P(), P()),
        check_vma=False,
    )
```

```python
import functools

import jax
import jax.numpy as jnp
from jax import lax
from jax.experimental import pallas as pl
from jax.experimental.pallas import tpu as pltpu
from jax.sharding import Mesh, PartitionSpec as P

AXES = ("yl", "z", "c", "yh", "x")
SIZES = (2, 8, 2, 2, 4)
DOM = ("yl", "z", "c")
PEERS = ("yl", "z")
REP = ("yh", "x")

TILE = 128
SLOTS = 32
HALF = SLOTS // 2
ROW_TILES = 8
NX = 4
NY = 4
NZ = 8
NP = 16
NR = 8
WIDE = 128
THIN = WIDE // NX
MAIN = ROW_TILES * THIN
BLOCK_HALF = ROW_TILES // 2
LAST = BLOCK_HALF * THIN
GRADS = THIN // 2
EXTRA = 32
SWAPS = 2
PARTS = 4
PIECE = NZ * LAST
META = 4 * SLOTS
RELAY_COST = pl.CostEstimate(flops=14 * 10**9, bytes_accessed=42 * 10**6, transcendentals=0)
UNROLL = 16

F32 = jnp.float32
BF16 = jnp.bfloat16
CONTRACT_LAST = (((1,), (1,)), ((), ()))
CONTRACT_FIRST = (((0,), (0,)), ((), ()))
PLAIN = (((1,), (0,)), ((), ()))


def mul(a, b, how):
    return lax.dot_general(a, b, how, preferred_element_type=F32)


def prep_kernel(ids, feat, out):
    first = ids[0] * THIN
    rows = lax.broadcasted_iota(jnp.int32, (THIN, WIDE), 0) + first
    cols = lax.broadcasted_iota(jnp.int32, (THIN, WIDE), 1)
    pick = (rows == cols).astype(BF16)
    for t in range(ROW_TILES):
        part = mul(pick, feat[t * TILE : (t + 1) * TILE, :], CONTRACT_LAST).astype(BF16)
        for p in range(NP):
            out[p, t * THIN : (t + 1) * THIN, :] = part


def every_slot(tile_refs, work):
    for ref, meta, skip in tile_refs:
        prods = [work(ref[s], meta, skip + s) for s in range(ref.shape[0])]
        for target, index, prod in prods:
            target[index] += prod


def relay_kernel(left, right, meta_l, meta_r, meta_f, out_a, out_b, out_l, out_r, out_f, sem):
    copies = []
    step = HALF // PARTS
    for k in range(PARTS):
        to = pl.ds(k * step, step)
        from_b = pl.ds(HALF + k * step, step)
        copies.append(pltpu.make_async_copy(left.at[to], out_a.at[to], sem.at[0, k]))
        copies.append(pltpu.make_async_copy(right.at[from_b], out_b.at[to], sem.at[1, k]))
    for copy in copies:
        copy.start()
    out_l[...] = meta_l[...]
    out_r[...] = meta_r[...]
    out_f[...] = meta_f[...]
    for copy in copies:
        copy.wait()


def fetch_far(far_a, far_b, far, far_sem):
    copies = [
        pltpu.make_async_copy(ref, far.at[k], far_sem.at[k]) for k, ref in enumerate((far_a, far_b))
    ]
    for copy in copies:
        copy.start()
    return copies


def forward_kernel(meta, meta_l, meta_r, meta_f, own, left, right, far_a, far_b, mine, *rest):
    others, (out, table, acc, far, far_sem) = rest[:SWAPS], rest[SWAPS:]
    fetch = fetch_far(far_a, far_b, far, far_sem)
    acc[...] = jnp.zeros_like(acc)
    half = NP * ROW_TILES
    table[0:half] = mine[...]
    for k, other in enumerate(others):
        per = half // SWAPS
        table[half + k * per : half + (k + 1) * per] = other[...]
    table[2 * half] = jnp.zeros((THIN, TILE), BF16)

    def work(tile, meta, s):
        return acc, meta[s], mul(tile, table[meta[SLOTS + s]], CONTRACT_LAST)

    every_slot([(own, meta, 0), (left, meta_l, 0), (right, meta_r, 0)], work)
    for copy in fetch:
        copy.wait()
    every_slot([(far.at[0], meta_f, 0), (far.at[1], meta_f, HALF)], work)
    for t in range(ROW_TILES):
        out[t] = acc[t].T


def backward_kernel(
    ids, meta, meta_l, meta_r, meta_f, own, left, right, far_a, far_b, agg, agg_l, agg_r, agg_f, weight, bias, cot,
    act, keep, *rest,
):
    send_a, send_b, acc, back, full, slopes, wsum, far, act_in, far_sem, act_sem = rest
    sends = {1: send_a.at[0], 2: send_a.at[1], 3: send_b.at[0], 0: send_b.at[1]}
    fetch = fetch_far(far_a, far_b, far, far_sem)
    x, yl, yh = ids[0], ids[2], ids[3]
    acc[...] = jnp.zeros_like(acc)
    for t in range(ROW_TILES):
        for k, part in ((0, agg), (1, agg_l), (3, agg_r), (2, agg_f)):
            full[t, pl.ds(pl.multiple_of(((x - k + NX) % NX) * THIN, THIN), THIN), :] = part[t]
    w_rows = weight[pl.ds(pl.multiple_of(x * THIN, THIN), THIN), :]
    for t in range(ROW_TILES):
        pre = mul(full[t], weight[...], CONTRACT_FIRST) + bias[...]
        sq = pre * pre
        th = jnp.tanh(0.7978845608028654 * pre * (1.0 + 0.044715 * sq))
        half = 0.5 * (1.0 + th)
        act_in[t * TILE : (t + 1) * TILE, :] = (pre * half).astype(BF16)
        slope = half + 0.5 * pre * (1.0 - th * th) * (
            0.7978845608028654 * (1.0 + (3 * 0.044715) * sq)
        )
        delta = (cot[t * TILE : (t + 1) * TILE, :].astype(F32) * slope).astype(BF16)
        slopes[t] = delta
        back[t] = mul(w_rows, delta, CONTRACT_LAST).astype(BF16)
    give = pltpu.make_async_copy(act_in, act, act_sem)
    give.start()
    bsum = jnp.zeros((1, WIDE), F32)
    wpart = jnp.zeros((THIN, WIDE), F32)
    for t in range(BLOCK_HALF):
        at = yh * BLOCK_HALF + t
        delta = slopes[at]
        wpart = wpart + mul(agg[at], delta, PLAIN)
        bsum = bsum + jnp.sum(delta.astype(F32), axis=0, keepdims=True)
    wsum[...] = wpart
    rest = jnp.where(
        lax.broadcasted_iota(jnp.int32, (EXTRA - GRADS, WIDE), 0) == 0,
        jnp.broadcast_to(bsum, (EXTRA - GRADS, WIDE)),
        0.0,
    )
    y = yh * 2 + yl
    for k in range(NY):
        there = ((y + k) % NY) // 2
        some = wsum[pl.ds(pl.multiple_of(there * GRADS, GRADS), GRADS), :]
        extra = jnp.concatenate([some, rest], axis=0).astype(BF16)
        keep[k, PIECE:, :] = extra
        sends[k][PIECE:, :] = extra

    back[ROW_TILES] = jnp.zeros((THIN, TILE), BF16)

    def work(tile, meta, s):
        return acc, meta[3 * SLOTS + s], mul(back[meta[2 * SLOTS + s]], tile, PLAIN)

    every_slot([(own, meta, 0), (left, meta_l, 0), (right, meta_r, 0)], work)
    for copy in fetch:
        copy.wait()
    every_slot([(far.at[0], meta_f, 0), (far.at[1], meta_f, HALF)], work)
    per = NZ * BLOCK_HALF
    for k in range(NY):
        for i in range(per):
            keep[k, i * THIN : (i + 1) * THIN, :] = acc[k * per + i].astype(BF16)
            sends[k][i * THIN : (i + 1) * THIN, :] = acc[(NY + k) * per + i].astype(BF16)
    give.wait()


def pair_kernel(which, keep, got, *outs):
    for at, (k, out) in enumerate(zip(which, outs)):
        out[...] = (keep[k].astype(F32) + got[at].astype(F32)).astype(BF16)


def y_sum_kernel(own, before, across, after, out):
    def total(rows):
        near = own[rows, :].astype(F32) + across[rows, :].astype(F32)
        return (near + (before[rows, :].astype(F32) + after[rows, :].astype(F32))).astype(BF16)

    extra = total(slice(PIECE, PIECE + EXTRA))
    for z in range(NZ):
        out[z, 0:LAST, :] = total(slice(z * LAST, (z + 1) * LAST))
        out[z, LAST:, :] = extra


def z_sum_kernel(got, out):
    total = got[0].astype(F32)
    for z in range(1, NZ):
        total = total + got[z].astype(F32)
    total = total.astype(BF16)
    for r in range(NR):
        out[r] = total


def finish_kernel(got, grad, wgrad, bgrad, blocks, sem):
    copies = []
    for t in range(ROW_TILES):
        first = (t // BLOCK_HALF) * NX
        at = (t % BLOCK_HALF) * THIN
        block = jnp.concatenate(
            [got[first + x, at : at + THIN, :].astype(F32) for x in range(NX)], axis=0
        )
        blocks[t] = block.T
        copies.append(
            pltpu.make_async_copy(blocks.at[t], grad.at[pl.ds(t * TILE, TILE)], sem.at[t])
        )
        copies[t].start()
    for yh in range(2):
        for x in range(NX):
            to = x * THIN + yh * GRADS
            wgrad[to : to + GRADS, :] = got[yh * NX + x, LAST : LAST + GRADS, :].astype(F32)
    bgrad[...] = got[0, LAST + GRADS : LAST + EXTRA, :].astype(F32)[0:1, :]
    for copy in copies:
        copy.wait()


def slot_meta(rows, cols, count, core, y):
    live = lax.broadcasted_iota(jnp.int32, rows.shape, 1) < count
    owner, block = cols // ROW_TILES, cols % ROW_TILES
    apart = jnp.where(owner % 2 == core, 0, 1)
    peer = owner // 2
    source = (apart * NP + peer) * ROW_TILES + block
    step = ((block // BLOCK_HALF) * 2 + peer // NZ - y + NY) % NY
    target = ((apart * NY + step) * NZ + peer % NZ) * BLOCK_HALF + block % BLOCK_HALF
    return jnp.concatenate(
        [
            rows,
            jnp.where(live, source, 2 * NP * ROW_TILES),
            jnp.where(live, rows, ROW_TILES),
            target,
        ],
        axis=1,
    )


def rotate(value, step):
    return lax.ppermute(value, "x", [(k, (k + step) % NX) for k in range(NX)])


def along_y(value, step):
    pairs = []
    for y in range(NY):
        to = (y + step) % NY
        pairs.append(((y % 2) * 2 + y // 2, (to % 2) * 2 + to // 2))
    return lax.ppermute(value, ("yl", "yh"), pairs)


def swap(value, axis):
    return lax.ppermute(value, axis, [(0, 1), (1, 0)])


def exchange(value, axes):
    return lax.all_to_all(value, axes, 0, 0, tiled=True)


def place(loose):
    return pl.BlockSpec(memory_space=pl.ANY if loose else pltpu.VMEM)


def kernel_call(body, name, outs, scalars, scratch, mb, *args, cost=None, loose_in=(), loose_out=()):
    one = isinstance(outs, tuple)
    shapes = [outs] if one else outs
    result = pl.pallas_call(
        body,
        out_shape=[jax.ShapeDtypeStruct(s, d) for s, d in shapes],
        grid_spec=pltpu.PrefetchScalarGridSpec(
            num_scalar_prefetch=scalars,
            grid=(),
            in_specs=[place(i in loose_in) for i in range(len(args) - scalars)],
            out_specs=[place(i in loose_out) for i in range(len(shapes))],
            scratch_shapes=scratch,
        ),
        compiler_params=pltpu.CompilerParams(vmem_limit_bytes=mb * 1024 * 1024),
        cost_estimate=cost,
        name=name,
    )(*args)
    return result[0] if one else result


def pair(which, keep, got):
    outs = [(got.shape[1:], BF16)] * 2
    return kernel_call(functools.partial(pair_kernel, which), "pair", outs, 0, [], 12, keep, got)


def shards(features, tile_values, tile_rows, tile_cols, tile_count, weight, bias, cotangent):
    x, core, yl, yh = (lax.axis_index(a).astype(jnp.int32) for a in ("x", "c", "yl", "yh"))
    ids = jnp.stack([x, core, yl, yh])
    own = tile_values[0, 0]
    left = rotate(own, 1)
    right = rotate(own, NX - 1)
    own_meta = slot_meta(tile_rows[0], tile_cols[0], tile_count, core, yh * 2 + yl)
    half = ((HALF, TILE, TILE), BF16)
    line = ((1, META), jnp.int32)
    pass_a, pass_b, *metas = kernel_call(
        relay_kernel,
        "relay",
        [half, half, line, line, line],
        0,
        [pltpu.SemaphoreType.DMA((2, PARTS))],
        6,
        left,
        right,
        rotate(own_meta, 1),
        rotate(own_meta, NX - 1),
        rotate(own_meta, 2),
        cost=RELAY_COST,
        loose_in=(0, 1),
        loose_out=(0, 1),
    )
    metas = [m.reshape(META) for m in (own_meta, *metas)]
    far_a, far_b = rotate(pass_a, 1), rotate(pass_b, NX - 1)
    tiles = (own, left, right, far_a, far_b)

    copies = kernel_call(prep_kernel, "prep", ((NP, MAIN, TILE), BF16), 1, [], 6, ids, features)
    mine = exchange(copies, PEERS)
    mine = mine.reshape(NP * ROW_TILES, THIN, TILE)
    per = NP * ROW_TILES // SWAPS
    others = [swap(mine[k * per : (k + 1) * per], "c") for k in range(SWAPS)]

    thin = (ROW_TILES, THIN, TILE)
    scratch = [
        pltpu.VMEM((2 * NP * ROW_TILES + 1, THIN, TILE), BF16),
        pltpu.VMEM((ROW_TILES, TILE, THIN), F32),
        pltpu.VMEM((2, HALF, TILE, TILE), BF16),
        pltpu.SemaphoreType.DMA((2,)),
    ]
    part = kernel_call(
        forward_kernel, "forward", (thin, F32), 4, scratch, 16, *metas, *tiles, mine, *others, loose_in=(3, 4)
    )
    agg = (part + swap(part, "yh")).astype(BF16)
    agg_l, agg_r, agg_f = rotate(agg, 1), rotate(agg, NX - 1), rotate(agg, 2)

    piece = PIECE + EXTRA
    square = (ROW_TILES, TILE, WIDE)
    activations, keep, send_a, send_b = kernel_call(
        backward_kernel,
        "backward",
        [((ROW_TILES * TILE, WIDE), BF16), ((NY, piece, TILE), BF16)] + [((2, piece, TILE), BF16)] * 2,
        5,
        [
            pltpu.VMEM((2 * NY * NZ * BLOCK_HALF, THIN, TILE), F32),
            pltpu.VMEM((ROW_TILES + 1, THIN, TILE), BF16),
            pltpu.VMEM(square, BF16),
            pltpu.VMEM(square, BF16),
            pltpu.VMEM((THIN, WIDE), F32),
            pltpu.VMEM((2, HALF, TILE, TILE), BF16),
            pltpu.VMEM((ROW_TILES * TILE, WIDE), BF16),
            pltpu.SemaphoreType.DMA((2,)),
            pltpu.SemaphoreType.DMA(()),
        ],
        20,
        ids,
        *metas,
        *tiles,
        agg,
        agg_l,
        agg_r,
        agg_f,
        weight,
        bias.reshape(1, WIDE),
        cotangent,
        loose_in=(3, 4),
        loose_out=(0,),
    )
    one, two = pair((1, 2), keep, swap(send_a, "c"))
    three, stay = pair((3, 0), keep, swap(send_b, "c"))
    before, across, after = along_y(one, 1), along_y(two, 2), along_y(three, 3)
    last = LAST + EXTRA
    summed = kernel_call(
        y_sum_kernel, "y_sum", ((NZ, last, TILE), BF16), 0, [], 12, stay, before, across, after
    )
    got = exchange(summed, "z")
    shared = kernel_call(z_sum_kernel, "z_sum", ((NR, last, TILE), BF16), 0, [], 16, got)
    got = exchange(shared, REP)
    feature_grad, weight_grad, bias_grad = kernel_call(
        finish_kernel,
        "finish",
        [((ROW_TILES * TILE, WIDE), F32), ((WIDE, WIDE), F32), ((1, WIDE), F32)],
        0,
        [pltpu.VMEM((ROW_TILES, TILE, WIDE), F32), pltpu.SemaphoreType.DMA((ROW_TILES,))],
        16,
        got,
        loose_out=(0,),
    )
    return (activations, feature_grad, weight_grad, bias_grad.reshape(WIDE))


def solution(mesh):
    fine = Mesh(mesh.devices.reshape(SIZES), AXES)
    return jax.shard_map(
        shards,
        mesh=fine,
        in_specs=(
            P(DOM, None),
            P(DOM, REP, None, None, None),
            P(DOM, REP, None),
            P(DOM, REP, None),
            P(DOM, REP),
            P(),
            P(),
            P(DOM, None),
        ),
        out_specs=(P(DOM, None), P(DOM, None), P(), P()),
        check_vma=False,
    )
```

```python
import functools

import jax
import jax.numpy as jnp
from jax import lax
from jax.experimental import pallas as pl
from jax.experimental.pallas import tpu as pltpu
from jax.sharding import Mesh, PartitionSpec as P

AXES = ("yl", "z", "c", "yh", "x")
SIZES = (2, 8, 2, 2, 4)
DOM = ("yl", "z", "c")
PEERS = ("yl", "z")
REP = ("yh", "x")

TILE = 128
SLOTS = 32
HALF = SLOTS // 2
ROW_TILES = 8
NX = 4
NY = 4
NZ = 8
NP = 16
NR = 8
WIDE = 128
THIN = WIDE // NX
MAIN = ROW_TILES * THIN
BLOCK_HALF = ROW_TILES // 2
LAST = BLOCK_HALF * THIN
GRADS = THIN // 2
EXTRA = 32
SWAPS = 2
PIECE = NZ * LAST
META = 4 * SLOTS
RELAY_COST = pl.CostEstimate(flops=14 * 10**9, bytes_accessed=42 * 10**6, transcendentals=0)
UNROLL = 16

F32 = jnp.float32
BF16 = jnp.bfloat16
CONTRACT_LAST = (((1,), (1,)), ((), ()))
CONTRACT_FIRST = (((0,), (0,)), ((), ()))
PLAIN = (((1,), (0,)), ((), ()))


def mul(a, b, how):
    return lax.dot_general(a, b, how, preferred_element_type=F32)


def prep_kernel(ids, feat, out):
    first = ids[0] * THIN
    rows = lax.broadcasted_iota(jnp.int32, (THIN, WIDE), 0) + first
    cols = lax.broadcasted_iota(jnp.int32, (THIN, WIDE), 1)
    pick = (rows == cols).astype(BF16)
    for t in range(ROW_TILES):
        part = mul(pick, feat[t * TILE : (t + 1) * TILE, :], CONTRACT_LAST).astype(BF16)
        for p in range(NP):
            out[p, t * THIN : (t + 1) * THIN, :] = part


def every_slot(tile_refs, work):
    for ref, meta, skip in tile_refs:
        prods = [work(ref[s], meta, skip + s) for s in range(ref.shape[0])]
        for target, index, prod in prods:
            target[index] += prod


def relay_kernel(left, right, meta_l, meta_r, meta_f, out_a, out_b, out_l, out_r, out_f):
    out_a[...] = left[0:HALF]
    out_b[...] = right[HALF:SLOTS]
    out_l[...] = meta_l[...]
    out_r[...] = meta_r[...]
    out_f[...] = meta_f[...]


def fetch_far(far_a, far_b, far, far_sem):
    copies = [
        pltpu.make_async_copy(ref, far.at[k], far_sem.at[k]) for k, ref in enumerate((far_a, far_b))
    ]
    for copy in copies:
        copy.start()
    return copies


def forward_kernel(meta, meta_l, meta_r, meta_f, own, left, right, far_a, far_b, mine, *rest):
    others, (out, table, acc, far, far_sem) = rest[:SWAPS], rest[SWAPS:]
    fetch = fetch_far(far_a, far_b, far, far_sem)
    acc[...] = jnp.zeros_like(acc)
    half = NP * ROW_TILES
    table[0:half] = mine[...]
    for k, other in enumerate(others):
        per = half // SWAPS
        table[half + k * per : half + (k + 1) * per] = other[...]
    table[2 * half] = jnp.zeros((THIN, TILE), BF16)

    def work(tile, meta, s):
        return acc, meta[s], mul(tile, table[meta[SLOTS + s]], CONTRACT_LAST)

    every_slot([(own, meta, 0), (left, meta_l, 0), (right, meta_r, 0)], work)
    for copy in fetch:
        copy.wait()
    every_slot([(far.at[0], meta_f, 0), (far.at[1], meta_f, HALF)], work)
    for t in range(ROW_TILES):
        out[t] = acc[t].T


def backward_kernel(
    ids, meta, meta_l, meta_r, meta_f, own, left, right, far_a, far_b, agg, agg_l, agg_r, agg_f, weight, bias, cot,
    act, keep, *rest,
):
    send_a, send_b, send_c, acc, back, full, slopes, wsum, far, act_in, far_sem, act_sem = rest
    sends = {1: send_a.at[0], 2: send_a.at[1], 3: send_b.at[0], 0: send_c.at[0]}
    fetch = fetch_far(far_a, far_b, far, far_sem)
    x, yl, yh = ids[0], ids[2], ids[3]
    acc[...] = jnp.zeros_like(acc)
    for t in range(ROW_TILES):
        for k, part in ((0, agg), (1, agg_l), (3, agg_r), (2, agg_f)):
            full[t, pl.ds(pl.multiple_of(((x - k + NX) % NX) * THIN, THIN), THIN), :] = part[t]
    w_rows = weight[pl.ds(pl.multiple_of(x * THIN, THIN), THIN), :]
    for t in range(ROW_TILES):
        pre = mul(full[t], weight[...], CONTRACT_FIRST) + bias[...]
        sq = pre * pre
        th = jnp.tanh(0.7978845608028654 * pre * (1.0 + 0.044715 * sq))
        half = 0.5 * (1.0 + th)
        act_in[t * TILE : (t + 1) * TILE, :] = (pre * half).astype(BF16)
        slope = half + 0.5 * pre * (1.0 - th * th) * (
            0.7978845608028654 * (1.0 + (3 * 0.044715) * sq)
        )
        delta = (cot[t * TILE : (t + 1) * TILE, :].astype(F32) * slope).astype(BF16)
        slopes[t] = delta
        back[t] = mul(w_rows, delta, CONTRACT_LAST).astype(BF16)
    give = pltpu.make_async_copy(act_in, act, act_sem)
    give.start()
    bsum = jnp.zeros((1, WIDE), F32)
    wpart = jnp.zeros((THIN, WIDE), F32)
    for t in range(BLOCK_HALF):
        at = yh * BLOCK_HALF + t
        delta = slopes[at]
        wpart = wpart + mul(agg[at], delta, PLAIN)
        bsum = bsum + jnp.sum(delta.astype(F32), axis=0, keepdims=True)
    wsum[...] = wpart
    rest = jnp.where(
        lax.broadcasted_iota(jnp.int32, (EXTRA - GRADS, WIDE), 0) == 0,
        jnp.broadcast_to(bsum, (EXTRA - GRADS, WIDE)),
        0.0,
    )
    y = yh * 2 + yl
    for k in range(NY):
        there = ((y + k) % NY) // 2
        some = wsum[pl.ds(pl.multiple_of(there * GRADS, GRADS), GRADS), :]
        extra = jnp.concatenate([some, rest], axis=0).astype(BF16)
        keep[k, PIECE:, :] = extra
        sends[k][PIECE:, :] = extra

    back[ROW_TILES] = jnp.zeros((THIN, TILE), BF16)

    def work(tile, meta, s):
        return acc, meta[3 * SLOTS + s], mul(back[meta[2 * SLOTS + s]], tile, PLAIN)

    every_slot([(own, meta, 0), (left, meta_l, 0), (right, meta_r, 0)], work)
    for copy in fetch:
        copy.wait()
    every_slot([(far.at[0], meta_f, 0), (far.at[1], meta_f, HALF)], work)
    per = NZ * BLOCK_HALF
    for k in range(NY):
        for i in range(per):
            keep[k, i * THIN : (i + 1) * THIN, :] = acc[k * per + i].astype(BF16)
            sends[k][i * THIN : (i + 1) * THIN, :] = acc[(NY + k) * per + i].astype(BF16)
    give.wait()


def pair_kernel(which, keep, got, *outs):
    for at, (k, out) in enumerate(zip(which, outs)):
        out[...] = (keep[k].astype(F32) + got[at].astype(F32)).astype(BF16)


def y_sum_kernel(keep, got, before, across, after, out):
    def total(rows):
        own = (keep[0, rows, :].astype(F32) + got[0, rows, :].astype(F32)).astype(BF16)
        near = own.astype(F32) + across[rows, :].astype(F32)
        return (near + (before[rows, :].astype(F32) + after[rows, :].astype(F32))).astype(BF16)

    extra = total(slice(PIECE, PIECE + EXTRA))
    for z in range(NZ):
        out[z, 0:LAST, :] = total(slice(z * LAST, (z + 1) * LAST))
        out[z, LAST:, :] = extra


def z_sum_kernel(got, out):
    total = got[0].astype(F32)
    for z in range(1, NZ):
        total = total + got[z].astype(F32)
    total = total.astype(BF16)
    for r in range(NR):
        out[r] = total


def finish_kernel(got, grad, wgrad, bgrad):
    for t in range(ROW_TILES):
        first = (t // BLOCK_HALF) * NX
        at = (t % BLOCK_HALF) * THIN
        block = jnp.concatenate(
            [got[first + x, at : at + THIN, :].astype(F32) for x in range(NX)], axis=0
        )
        grad[t * TILE : (t + 1) * TILE, :] = block.T
    for yh in range(2):
        for x in range(NX):
            to = x * THIN + yh * GRADS
            wgrad[to : to + GRADS, :] = got[yh * NX + x, LAST : LAST + GRADS, :].astype(F32)
    bgrad[...] = got[0, LAST + GRADS : LAST + EXTRA, :].astype(F32)[0:1, :]


def slot_meta(rows, cols, count, core, y):
    live = lax.broadcasted_iota(jnp.int32, rows.shape, 1) < count
    owner, block = cols // ROW_TILES, cols % ROW_TILES
    apart = jnp.where(owner % 2 == core, 0, 1)
    peer = owner // 2
    source = (apart * NP + peer) * ROW_TILES + block
    step = ((block // BLOCK_HALF) * 2 + peer // NZ - y + NY) % NY
    target = ((apart * NY + step) * NZ + peer % NZ) * BLOCK_HALF + block % BLOCK_HALF
    return jnp.concatenate(
        [
            rows,
            jnp.where(live, source, 2 * NP * ROW_TILES),
            jnp.where(live, rows, ROW_TILES),
            target,
        ],
        axis=1,
    )


def rotate(value, step):
    return lax.ppermute(value, "x", [(k, (k + step) % NX) for k in range(NX)])


def along_y(value, step):
    pairs = []
    for y in range(NY):
        to = (y + step) % NY
        pairs.append(((y % 2) * 2 + y // 2, (to % 2) * 2 + to // 2))
    return lax.ppermute(value, ("yl", "yh"), pairs)


def swap(value, axis):
    return lax.ppermute(value, axis, [(0, 1), (1, 0)])


def exchange(value, axes):
    return lax.all_to_all(value, axes, 0, 0, tiled=True)


def place(loose):
    return pl.BlockSpec(memory_space=pl.ANY if loose else pltpu.VMEM)


def kernel_call(body, name, outs, scalars, scratch, mb, *args, cost=None, loose_in=(), loose_out=()):
    one = isinstance(outs, tuple)
    shapes = [outs] if one else outs
    result = pl.pallas_call(
        body,
        out_shape=[jax.ShapeDtypeStruct(s, d) for s, d in shapes],
        grid_spec=pltpu.PrefetchScalarGridSpec(
            num_scalar_prefetch=scalars,
            grid=(),
            in_specs=[place(i in loose_in) for i in range(len(args) - scalars)],
            out_specs=[place(i in loose_out) for i in range(len(shapes))],
            scratch_shapes=scratch,
        ),
        compiler_params=pltpu.CompilerParams(vmem_limit_bytes=mb * 1024 * 1024),
        cost_estimate=cost,
        name=name,
    )(*args)
    return result[0] if one else result


def pair(which, keep, got):
    outs = [(got.shape[1:], BF16)] * len(which)
    return kernel_call(functools.partial(pair_kernel, which), "pair", outs, 0, [], 12, keep, got)


def shards(features, tile_values, tile_rows, tile_cols, tile_count, weight, bias, cotangent):
    x, core, yl, yh = (lax.axis_index(a).astype(jnp.int32) for a in ("x", "c", "yl", "yh"))
    ids = jnp.stack([x, core, yl, yh])
    own = tile_values[0, 0]
    left = rotate(own, 1)
    right = rotate(own, NX - 1)
    own_meta = slot_meta(tile_rows[0], tile_cols[0], tile_count, core, yh * 2 + yl)
    half = ((HALF, TILE, TILE), BF16)
    line = ((1, META), jnp.int32)
    pass_a, pass_b, *metas = kernel_call(
        relay_kernel,
        "relay",
        [half, half, line, line, line],
        0,
        [],
        6,
        left,
        right,
        rotate(own_meta, 1),
        rotate(own_meta, NX - 1),
        rotate(own_meta, 2),
        cost=RELAY_COST,
    )
    metas = [m.reshape(META) for m in (own_meta, *metas)]
    far_a, far_b = rotate(pass_a, 1), rotate(pass_b, NX - 1)
    tiles = (own, left, right, far_a, far_b)

    copies = kernel_call(prep_kernel, "prep", ((NP, MAIN, TILE), BF16), 1, [], 6, ids, features)
    mine = exchange(copies, PEERS)
    mine = mine.reshape(NP * ROW_TILES, THIN, TILE)
    per = NP * ROW_TILES // SWAPS
    others = [swap(mine[k * per : (k + 1) * per], "c") for k in range(SWAPS)]

    thin = (ROW_TILES, THIN, TILE)
    scratch = [
        pltpu.VMEM((2 * NP * ROW_TILES + 1, THIN, TILE), BF16),
        pltpu.VMEM((ROW_TILES, TILE, THIN), F32),
        pltpu.VMEM((2, HALF, TILE, TILE), BF16),
        pltpu.SemaphoreType.DMA((2,)),
    ]
    part = kernel_call(
        forward_kernel, "forward", (thin, F32), 4, scratch, 16, *metas, *tiles, mine, *others, loose_in=(3, 4)
    )
    agg = (part + swap(part, "yh")).astype(BF16)
    agg_l, agg_r, agg_f = rotate(agg, 1), rotate(agg, NX - 1), rotate(agg, 2)

    piece = PIECE + EXTRA
    square = (ROW_TILES, TILE, WIDE)
    activations, keep, send_a, send_b, send_c = kernel_call(
        backward_kernel,
        "backward",
        [((ROW_TILES * TILE, WIDE), BF16), ((NY, piece, TILE), BF16)]
        + [((n, piece, TILE), BF16) for n in (2, 1, 1)],
        5,
        [
            pltpu.VMEM((2 * NY * NZ * BLOCK_HALF, THIN, TILE), F32),
            pltpu.VMEM((ROW_TILES + 1, THIN, TILE), BF16),
            pltpu.VMEM(square, BF16),
            pltpu.VMEM(square, BF16),
            pltpu.VMEM((THIN, WIDE), F32),
            pltpu.VMEM((2, HALF, TILE, TILE), BF16),
            pltpu.VMEM((ROW_TILES * TILE, WIDE), BF16),
            pltpu.SemaphoreType.DMA((2,)),
            pltpu.SemaphoreType.DMA(()),
        ],
        20,
        ids,
        *metas,
        *tiles,
        agg,
        agg_l,
        agg_r,
        agg_f,
        weight,
        bias.reshape(1, WIDE),
        cotangent,
        loose_in=(3, 4),
        loose_out=(0,),
    )
    one, two = pair((1, 2), keep, swap(send_a, "c"))
    (three,) = pair((3,), keep, swap(send_b, "c"))
    stay = swap(send_c, "c")
    before, across, after = along_y(one, 1), along_y(two, 2), along_y(three, 3)
    last = LAST + EXTRA
    summed = kernel_call(
        y_sum_kernel, "y_sum", ((NZ, last, TILE), BF16), 0, [], 12, keep, stay, before, across, after
    )
    got = exchange(summed, "z")
    shared = kernel_call(z_sum_kernel, "z_sum", ((NR, last, TILE), BF16), 0, [], 16, got)
    got = exchange(shared, REP)
    feature_grad, weight_grad, bias_grad = kernel_call(
        finish_kernel,
        "finish",
        [((ROW_TILES * TILE, WIDE), F32), ((WIDE, WIDE), F32), ((1, WIDE), F32)],
        0,
        [],
        16,
        got,
    )
    return (activations, feature_grad, weight_grad, bias_grad.reshape(WIDE))


def solution(mesh):
    fine = Mesh(mesh.devices.reshape(SIZES), AXES)
    return jax.shard_map(
        shards,
        mesh=fine,
        in_specs=(
            P(DOM, None),
            P(DOM, REP, None, None, None),
            P(DOM, REP, None),
            P(DOM, REP, None),
            P(DOM, REP),
            P(),
            P(),
            P(DOM, None),
        ),
        out_specs=(P(DOM, None), P(DOM, None), P(), P()),
        check_vma=False,
    )
```
